32 devices in a mesh: geom: 2 (over x), occ: 16 (over z, y, core).
Axes of the slice: x: 2, y: 2, z: 4, core: 2. Of those that a mesh axis runs over, the one named last changes fastest.
Arguments:
- three_index: bfloat16 [32, 512, 2048], P(('geom', 'occ')), parts along dimension 0, may hold values from -0.59765625 to 0.59765625
- occ_energy: float32 [32], P(('geom', 'occ')), parts along dimension 0, may hold values from -1.5 to -0.5
- vir_energy: float32 [1024], P('geom'), parts along dimension 0, may hold values from 0.5 to 3
Outputs:
- aux_density: bfloat16 [32, 512, 2048], P(('geom', 'occ')), parts along dimension 0
- vir_density: float32 [1024, 512], P(('geom', 'occ')), parts along dimension 0
The draws below stay inside these ranges and needn't reach their ends.
There are 2 independent parts, one for each index of `geom`. The reference program is written for one: setup_inputs(seed, part) draws one part's arguments, and reference() takes and returns one part's arrays. A program takes and returns all parts, laid end to end along the dimension named above; each array names one. Nothing has to cross between parts.
All inputs are finite; a program needn't handle non-finite values.
Results may differ from the reference program's by a relative error of at most 0.0055.
Values may be sent and summed in bfloat16 or wider, within the bound.
A program may use at most 64 MiB of HBM per device.

```python
import jax
import jax.numpy as jnp
from jax import lax

VIR = 512
NAUX = 2048
OCC_DEV = 1
REACH = 2
OCC = 16
N_OCC = 16


def block_scale(stream_key, dims, pieces, smallest, top_value):
    loudness = 1.0
    for position, parts in pieces:
        draws = jax.random.uniform(jax.random.fold_in(jax.random.fold_in(stream_key, 6), position), (parts,), jnp.float32, smallest / len(pieces), top_value / len(pieces))
        loudness = loudness * jnp.repeat(jnp.exp(draws), dims[position] // parts).reshape((-1,) + (1,) * (len(dims) - 1 - position))
    return loudness


def normal_values(own_key, dims, deviation, most, pieces=(), kind=jnp.bfloat16):
    array = deviation * jax.random.normal(own_key, dims, jnp.float32)
    if pieces:
        array = array * block_scale(own_key, dims, pieces, -0.22, 0.18)
    return jnp.clip(array, -most, most).astype(kind)


def setup_inputs(seed: int = 0, part: int = 0) -> dict:
    streams_of = jax.random.split(jax.random.key(seed), 4)
    part_keys = jax.random.split(jax.random.fold_in(streams_of[3], part), 4)
    return {
        "three_index": normal_values(part_keys[0], (OCC, VIR, NAUX), 0.1, 0.59765625, ((0, 16),)),
        "occ_energy": jnp.clip(-1.5 + 1.0 * jax.random.uniform(part_keys[1], (OCC,), jnp.float32) ** block_scale(part_keys[1], (OCC,), ((0, 16),), -0.2, 0.2), -1.5, -0.5),
        "vir_energy": jnp.clip(jax.random.uniform(part_keys[2], (VIR,), jnp.float32, 0.5, 3.0), 0.5, 3.0),
    }


def pair_terms(carry, own, own_eps, other, other_eps, vir_energy):
    density, vir_density = carry
    coulomb = jnp.einsum("iap,jbp->ijab", own.astype(jnp.float32), other.astype(jnp.float32))
    divisor = own_eps[:, None, None, None] + other_eps[None, :, None, None] - vir_energy[None, None, :, None] - vir_energy[None, None, None, :]
    amplitude = coulomb / divisor
    mixed = (2.0 * amplitude - jnp.swapaxes(amplitude, 2, 3)).astype(jnp.bfloat16)
    amp_half = amplitude.astype(jnp.bfloat16)
    density = density + jnp.einsum("ijab,jbp->iap", mixed.astype(jnp.float32), other.astype(jnp.float32))
    vir_density = vir_density + jnp.einsum("ijac,ijbc->ab", amp_half.astype(jnp.float32), mixed.astype(jnp.float32))
    return density, vir_density


def reference(three_index, occ_energy, vir_energy):
    blocks = three_index.reshape(N_OCC, OCC_DEV, VIR, NAUX)
    energies = occ_energy.reshape(N_OCC, OCC_DEV)

    def one_device(owner):
        own = blocks[owner]
        own_eps = energies[owner]
        carry = (jnp.zeros((OCC_DEV, VIR, NAUX), jnp.float32), jnp.zeros((VIR, VIR), jnp.float32))
        for offset in range(-REACH, REACH + 1):
            partner = ((owner + offset) % N_OCC).astype(jnp.int32)
            other = lax.dynamic_index_in_dim(blocks, partner, 0, keepdims=False)
            other_eps = lax.dynamic_index_in_dim(energies, partner, 0, keepdims=False)
            carry = pair_terms(carry, own, own_eps, other, other_eps, vir_energy)
        return carry[0].astype(jnp.bfloat16), carry[1]

    densities, vir_parts = lax.map(one_device, jnp.arange(N_OCC, dtype=jnp.int32))
    aux_density = densities.reshape(OCC, VIR, NAUX)
    vir_density = jnp.sum(vir_parts, axis=0) * (2.0 / (OCC * (2 * REACH + 1)))
    return aux_density, vir_density
```

```python
import functools

import jax
import jax.numpy as jnp
from jax import lax
from jax.experimental import pallas as pl
from jax.experimental.pallas import tpu as pltpu
from jax.sharding import PartitionSpec as P

MESH = pl.DeviceIdType.MESH
REACH = 2
CHUNKS = 16
WINDOW = 3
LAG = 3
NT = (((1,), (1,)), ((), ()))
Y, Z, S = 0, 1, 2


def kernel(
    n, x_ref, eps_ref, vir_ref, aux_ref, out_ref,
    mate, far, eps, base, coul, half, mixed, acc, vacc, r1, t2s, t2r, keep, t3s, t3r,
    e_send, e_recv, m_send, m_recv, y_send, y_recv, z_send, z_recv, s_send, s_recv, v_send, v_recv, p_send, p_recv,
):
    nvir, naux = x_ref.shape
    rows = nvir // n
    peers = n // 4
    me = lax.axis_index("occ")
    core = lax.rem(me, 2)
    chip = me // 2
    side = lax.rem(chip, 2)
    row = chip // 2
    mate_id = me + 1 - 2 * core
    y_id = me + 2 - 4 * side
    z_id = lax.rem(me + 4 - 8 * side + n, n)
    share = lax.rem(side + core, 2)

    barrier = pltpu.get_barrier_semaphore()
    others = [mate_id, y_id] + [lax.rem(me + 4 * d, n) for d in range(1, peers)]
    for other in others:
        pl.semaphore_signal(barrier, inc=1, device_id={"occ": other}, device_id_type=MESH)
    eps[0] = jnp.full(eps.shape[1:], eps_ref[0], jnp.float32)
    pl.semaphore_wait(barrier, len(others))

    def remote(src, dst, send, recv, to):
        return pltpu.make_async_remote_copy(
            src_ref=src, dst_ref=dst, send_sem=send, recv_sem=recv,
            device_id={"occ": to}, device_id_type=MESH,
        )

    step = nvir // CHUNKS

    def piece(r):
        return pl.ds(r * step, step)

    y_copy = [remote(x_ref.at[piece(r)], far.at[Y, piece(r)], y_send.at[r], y_recv.at[r], y_id) for r in range(CHUNKS)]
    z_copy = [remote(far.at[Y, piece(r)], far.at[Z, piece(r)], z_send.at[r], z_recv.at[r], z_id) for r in range(CHUNKS)]
    s_copy = [remote(far.at[share, piece(r)], far.at[S, piece(r)], s_send.at[r], s_recv.at[r], mate_id) for r in range(CHUNKS)]
    m_copy = remote(x_ref, mate, m_send, m_recv, mate_id)
    e_mate = remote(eps.at[0], eps.at[1], e_send.at[0], e_recv.at[0], mate_id)
    e_y = remote(eps.at[0], eps.at[2], e_send.at[1], e_recv.at[1], y_id)
    e_z = remote(eps.at[2], eps.at[3], e_send.at[2], e_recv.at[2], z_id)
    e_s = remote(eps.at[2 + share], eps.at[4], e_send.at[3], e_recv.at[3], mate_id)

    e_y.start()
    for r in range(WINDOW):
        y_copy[r].start()
    e_mate.start()
    m_copy.start()

    across = jnp.broadcast_to(vir_ref[...], (128, nvir))
    down = across.T
    for t in range(nvir // 128):
        base[:, pl.ds(t * 128, 128)] = -down - across[0:1, t * 128 : (t + 1) * 128]

    def coulomb(block, slot, first, count):
        for b in range(first, first + count):
            bs = pl.ds(b * 256, 256)
            coul[slot, :, bs] = lax.dot_general(x_ref[...], block[bs, :], NT, preferred_element_type=jnp.float32)

    def amplitudes(slot, which, fresh=False):
        level = eps[0, 0:1, :] + eps[which, 0:1, :]
        for t in range(nvir // 128):
            rs = pl.ds(t * 128, 128)
            value = coul[slot, rs, :] / (base[rs, :] + level)
            coul[slot, rs, :] = value
            half[rs, :] = value.astype(jnp.bfloat16)
        for t in range(nvir // 128):
            rs = pl.ds(t * 128, 128)
            mixed[slot, rs, :] = (2.0 * coul[slot, rs, :] - coul[slot, :, rs].T).astype(jnp.bfloat16)
        for t in range(2):
            part = lax.dot_general(
                half[pl.ds(t * (nvir // 2), nvir // 2), :], mixed[slot], NT, preferred_element_type=jnp.float32
            ).reshape(peers // 2, 2, 2, rows, nvir)
            hs = pl.ds(t * (peers // 2), peers // 2)
            vacc[hs] = part if fresh else vacc[hs] + part

    def density(block, slot, fresh=False, last=False):
        @pl.loop(0, naux // 256)
        def _(t):
            cs = pl.ds(pl.multiple_of(t * 256, 256), 256)
            part = jnp.dot(mixed[slot], block[:, cs], preferred_element_type=jnp.float32)
            if not fresh:
                part = acc[:, cs] + part
            if last:
                aux_ref[:, cs] = part.astype(aux_ref.dtype)
            else:
                acc[:, cs] = part

    def await_s(first, last):
        for r in range(first, last):
            s_copy[r].wait_recv()

    def mate_coulomb():
        m_copy.wait_recv()
        e_mate.wait_recv()
        coulomb(mate, 1, 0, 2)

    def s_first():
        await_s(0, CHUNKS // 2)
        coulomb(far.at[S], S, 0, 1)

    def y_last():
        coulomb(far.at[Y], Y, 1, 1)
        amplitudes(Y, 2)

    work = {
        0: lambda: coulomb(x_ref, 0, 0, 2),
        1: lambda: amplitudes(0, 0, fresh=True),
        2: lambda: density(x_ref, 0, fresh=True),
        4: mate_coulomb,
        5: lambda: amplitudes(1, 1),
        6: lambda: density(mate, 1),
        CHUNKS // 2: lambda: coulomb(far.at[Y], Y, 0, 1),
        CHUNKS // 2 + LAG: lambda: coulomb(far.at[Z], Z, 0, 1),
        CHUNKS // 2 + LAG + 2: s_first,
        CHUNKS: y_last,
        CHUNKS + 1: lambda: density(far.at[Y], Y),
    }
    for r in range(CHUNKS + LAG):
        if r < CHUNKS:
            y_copy[r].wait_recv()
            z_copy[r].start()
            if r + WINDOW < CHUNKS:
                y_copy[r + WINDOW].start()
        if r == 0:
            e_y.wait_recv()
            e_z.start()
        if r >= LAG:
            z_copy[r - LAG].wait_recv()
            s_copy[r - LAG].start()
        if r == LAG:
            e_z.wait_recv()
            e_s.start()
        if r in work:
            work[r]()

    coulomb(far.at[Z], Z, 1, 1)
    amplitudes(Z, 3)
    await_s(CHUNKS // 2, CHUNKS)
    e_s.wait_recv()
    coulomb(far.at[S], S, 1, 1)
    amplitudes(S, 4)

    v1 = remote(vacc.at[:, :, 1 - core], r1, v_send.at[0], v_recv.at[0], mate_id)
    v1.start()
    density(far.at[Z], Z)
    v1.wait_recv()
    t2s[...] = (vacc[:, 1 - side, core] + r1[:, 1 - side]).reshape(peers * rows, nvir).astype(t2s.dtype)
    v2 = remote(t2s, t2r, v_send.at[1], v_recv.at[1], y_id)
    v2.start()
    keep[...] = vacc[:, side, core] + r1[:, side]
    density(far.at[S], S, last=True)
    v2.wait_recv()
    total = keep[...] + t2r[...].astype(jnp.float32).reshape(peers, rows, nvir)
    keep[...] = total
    t3s[...] = total.astype(t3s.dtype)
    v3 = [
        remote(
            t3s.at[lax.rem(row + d, peers)], t3r.at[d - 1], p_send.at[d - 1], p_recv.at[d - 1], lax.rem(me + 4 * d, n)
        )
        for d in range(1, peers)
    ]
    for copy in v3:
        copy.start()
    result = keep[row]
    for d, copy in enumerate(v3):
        copy.wait_recv()
        result = result + t3r[d].astype(jnp.float32)
    out_ref[...] = result * (2.0 / (n * (2 * REACH + 1)))

    for copy in [e_mate, e_y, e_z, e_s, m_copy, *y_copy, *z_copy, *s_copy, v1, v2, *v3]:
        copy.wait_send()


def per_device(n, three_index, occ_energy, vir_energy):
    count, nvir, naux = three_index.shape
    rows, peers = nvir // n, n // 4
    narrow = jnp.bfloat16 if rows % 16 == 0 else jnp.float32
    f32, bf16, dma = jnp.float32, jnp.bfloat16, pltpu.SemaphoreType.DMA
    pairs = 2 * REACH + 1
    vmem = pl.BlockSpec(memory_space=pltpu.VMEM)
    aux, vir = pl.pallas_call(
        functools.partial(kernel, n),
        out_shape=(jax.ShapeDtypeStruct((nvir, naux), bf16), jax.ShapeDtypeStruct((rows, nvir), f32)),
        in_specs=[vmem, pl.BlockSpec(memory_space=pltpu.SMEM), vmem],
        out_specs=(vmem, vmem),
        scratch_shapes=[
            pltpu.VMEM((nvir, naux), bf16),
            pltpu.VMEM((3, nvir, naux), bf16),
            pltpu.VMEM((pairs, 8, nvir), f32),
            pltpu.VMEM((nvir, nvir), f32),
            pltpu.VMEM((3, nvir, nvir), f32),
            pltpu.VMEM((nvir, nvir), bf16),
            pltpu.VMEM((3, nvir, nvir), bf16),
            pltpu.VMEM((nvir, naux), f32),
            pltpu.VMEM((peers, 2, 2, rows, nvir), f32),
            pltpu.VMEM((peers, 2, rows, nvir), f32),
            pltpu.VMEM((peers * rows, nvir), bf16),
            pltpu.VMEM((peers * rows, nvir), bf16),
            pltpu.VMEM((peers, rows, nvir), f32),
            pltpu.VMEM((peers, rows, nvir), narrow),
            pltpu.VMEM((peers - 1, rows, nvir), narrow),
            dma((4,)), dma((4,)), dma, dma,
            dma((CHUNKS,)), dma((CHUNKS,)), dma((CHUNKS,)), dma((CHUNKS,)), dma((CHUNKS,)), dma((CHUNKS,)),
            dma((2,)), dma((2,)), dma((peers - 1,)), dma((peers - 1,)),
        ],
        compiler_params=pltpu.CompilerParams(
            collective_id=0, has_side_effects=True, vmem_limit_bytes=48 * 2**20
        ),
        cost_estimate=pl.CostEstimate(
            flops=pairs * (4 * nvir * nvir * naux + 2 * nvir**3), bytes_accessed=4 * nvir * naux, transcendentals=0
        ),
    )(three_index.reshape(nvir, naux), occ_energy, vir_energy.reshape(1, nvir))
    return aux.reshape(three_index.shape), vir


def solution(mesh):
    placed = (P(("geom", "occ"), None, None), P(("geom", "occ")), P("geom"))
    return jax.shard_map(
        functools.partial(per_device, mesh.shape["occ"]),
        mesh=mesh,
        in_specs=placed,
        out_specs=(P(("geom", "occ"), None, None), P(("geom", "occ"), None)),
        check_vma=False,
    )
```

```python
import functools

import jax
import jax.numpy as jnp
from jax import lax
from jax.experimental import pallas as pl
from jax.experimental.pallas import tpu as pltpu
from jax.sharding import PartitionSpec as P

MESH = pl.DeviceIdType.MESH
REACH = 2
WINDOW = 3
LAG = 3
NT = (((1,), (1,)), ((), ()))
Y, Z, S = 0, 1, 2


def cuts(nvir):
    small = [(first, 16) for first in range(nvir - 64, nvir, 16)]
    return [(first, 32) for first in range(0, nvir - 64, 32)] + small


def kernel(
    n, x_hbm, eps_ref, vir_hbm, aux_ref, out_ref,
    x_ref, vir_ref, mate, far, eps, base, coul, half, mixed, acc, vacc, r1, t2s, t2r, keep, t3s, t3r,
    e_send, e_recv, m_send, m_recv, y_send, y_recv, z_send, z_recv, s_send, s_recv, v_send, v_recv, p_send, p_recv, l_sem,
):
    nvir, naux = x_ref.shape
    rows = nvir // n
    peers = n // 4
    me = lax.axis_index("occ")
    core = lax.rem(me, 2)
    chip = me // 2
    side = lax.rem(chip, 2)
    row = chip // 2
    mate_id = me + 1 - 2 * core
    y_id = me + 2 - 4 * side
    z_id = lax.rem(me + 4 - 8 * side + n, n)
    share = lax.rem(side + core, 2)

    local = pltpu.make_async_copy(x_hbm, x_ref, l_sem.at[0])
    local_vir = pltpu.make_async_copy(vir_hbm, vir_ref, l_sem.at[1])
    local.start()
    local_vir.start()
    barrier = pltpu.get_barrier_semaphore()
    others = [mate_id, y_id] + [lax.rem(me + 4 * d, n) for d in range(1, peers)]
    for other in others:
        pl.semaphore_signal(barrier, inc=1, device_id={"occ": other}, device_id_type=MESH)
    eps[0] = jnp.full(eps.shape[1:], eps_ref[0], jnp.float32)
    pl.semaphore_wait(barrier, len(others))

    def remote(src, dst, send, recv, to):
        return pltpu.make_async_remote_copy(
            src_ref=src, dst_ref=dst, send_sem=send, recv_sem=recv,
            device_id={"occ": to}, device_id_type=MESH,
        )

    pieces = cuts(nvir)
    total_pieces = len(pieces)

    def piece(r):
        return pl.ds(*pieces[r])

    y_copy = [remote(x_hbm.at[piece(r)], far.at[Y, piece(r)], y_send.at[r], y_recv.at[r], y_id) for r in range(total_pieces)]
    z_copy = [remote(far.at[Y, piece(r)], far.at[Z, piece(r)], z_send.at[r], z_recv.at[r], z_id) for r in range(total_pieces)]
    s_copy = [remote(far.at[share, piece(r)], far.at[S, piece(r)], s_send.at[r], s_recv.at[r], mate_id) for r in range(total_pieces)]
    m_copy = remote(x_hbm, mate, m_send, m_recv, mate_id)
    e_mate = remote(eps.at[0], eps.at[1], e_send.at[0], e_recv.at[0], mate_id)
    e_y = remote(eps.at[0], eps.at[2], e_send.at[1], e_recv.at[1], y_id)
    e_z = remote(eps.at[2], eps.at[3], e_send.at[2], e_recv.at[2], z_id)
    e_s = remote(eps.at[2 + share], eps.at[4], e_send.at[3], e_recv.at[3], mate_id)

    e_y.start()
    for r in range(WINDOW):
        y_copy[r].start()
    e_mate.start()
    m_copy.start()

    local_vir.wait()
    across = jnp.broadcast_to(vir_ref[...], (128, nvir))
    down = across.T
    for t in range(nvir // 128):
        base[:, pl.ds(t * 128, 128)] = -down - across[0:1, t * 128 : (t + 1) * 128]

    def coulomb(block, slot, first, count):
        for b in range(first, first + count):
            bs = pl.ds(b * 256, 256)
            coul[slot, :, bs] = lax.dot_general(x_ref[...], block[bs, :], NT, preferred_element_type=jnp.float32)

    def amplitudes(slot, which, fresh=False):
        level = eps[0, 0:1, :] + eps[which, 0:1, :]
        for t in range(nvir // 128):
            rs = pl.ds(t * 128, 128)
            value = coul[slot, rs, :] / (base[rs, :] + level)
            coul[slot, rs, :] = value
            half[slot, rs, :] = value.astype(jnp.bfloat16)
        for t in range(nvir // 128):
            rs = pl.ds(t * 128, 128)
            mixed[slot, rs, :] = (2.0 * coul[slot, rs, :] - coul[slot, :, rs].T).astype(jnp.bfloat16)
        gather_vir(slot, fresh)

    def gather_vir(slot, fresh=False):
        for t in range(2):
            part = lax.dot_general(
                half[slot, pl.ds(t * (nvir // 2), nvir // 2), :], mixed[slot], NT, preferred_element_type=jnp.float32
            ).reshape(peers // 2, 2, 2, rows, nvir)
            hs = pl.ds(t * (peers // 2), peers // 2)
            vacc[hs] = part if fresh else vacc[hs] + part

    def quarter(slot, q):
        block = far.at[slot]
        cs = pl.ds(q * 128, 128)
        level = eps[0, 0:1, 0:128] + eps[2 + slot, 0:1, 0:128]
        value = lax.dot_general(x_ref[...], block[cs, :], NT, preferred_element_type=jnp.float32)
        value = value / (base[:, cs] + level)
        coul[slot, :, cs] = value
        half[slot, :, cs] = value.astype(jnp.bfloat16)
        for t in range(q + 1):
            ts = pl.ds(t * 128, 128)
            lower = coul[slot, cs, ts]
            upper = coul[slot, ts, cs]
            mixed[slot, cs, ts] = (2.0 * lower - upper.T).astype(jnp.bfloat16)
            if t < q:
                mixed[slot, ts, cs] = (2.0 * upper - lower.T).astype(jnp.bfloat16)

    def density(block, slot, fresh=False, last=False):
        @pl.loop(0, naux // 256)
        def _(t):
            cs = pl.ds(pl.multiple_of(t * 256, 256), 256)
            part = jnp.dot(mixed[slot], block[:, cs], preferred_element_type=jnp.float32)
            if not fresh:
                part = acc[:, cs] + part
            if last:
                aux_ref[:, cs] = part.astype(aux_ref.dtype)
            else:
                acc[:, cs] = part

    def first_of(q):
        return [r for r in range(total_pieces) if pieces[r][0] // 128 == q]

    def await_s(q):
        for r in first_of(q):
            s_copy[r].wait_recv()

    def mate_coulomb():
        m_copy.wait_recv()
        e_mate.wait_recv()
        coulomb(mate, 1, 0, 2)

    def self_coulomb():
        local.wait()
        coulomb(x_ref, 0, 0, 2)

    def shared(q):
        await_s(q)
        if q == 0:
            e_s.wait_recv()
        quarter(S, q)

    def y_last():
        quarter(Y, 3)
        gather_vir(Y)

    work = {
        0: self_coulomb,
        1: lambda: amplitudes(0, 0, fresh=True),
        2: lambda: density(x_ref, 0, fresh=True),
        3: mate_coulomb,
        4: lambda: amplitudes(1, 1),
        5: lambda: density(mate, 1),
        6: lambda: quarter(Y, 0),
        7: lambda: quarter(Z, 0),
        8: lambda: quarter(Y, 1),
        9: lambda: shared(0),
        11: lambda: quarter(Z, 1),
        12: lambda: quarter(Y, 2),
        13: lambda: shared(1),
        15: lambda: quarter(Z, 2),
        17: lambda: shared(2),
        total_pieces: y_last,
    }
    for r in range(total_pieces + LAG):
        if r < total_pieces:
            y_copy[r].wait_recv()
            z_copy[r].start()
            if r + WINDOW < total_pieces:
                y_copy[r + WINDOW].start()
        if r == 0:
            e_y.wait_recv()
            e_z.start()
        if r >= LAG:
            z_copy[r - LAG].wait_recv()
            s_copy[r - LAG].start()
        if r == LAG:
            e_z.wait_recv()
            e_s.start()
        if r in work:
            work[r]()

    quarter(Z, 3)
    gather_vir(Z)
    shared(3)
    gather_vir(S)

    sides = [pl.ds(k * (nvir // 2), nvir // 2) for k in range(2)]
    v1 = [
        remote(vacc.at[:, :, 1 - core, :, cs], r1.at[:, :, :, cs], v_send.at[k], v_recv.at[k], mate_id)
        for k, cs in enumerate(sides)
    ]
    v2 = [remote(t2s.at[k], t2r.at[k], v_send.at[2 + k], v_recv.at[2 + k], y_id) for k in range(2)]
    v3 = [
        [
            remote(
                t3s.at[k, lax.rem(row + d, peers)], t3r.at[k, d - 1],
                p_send.at[k, d - 1], p_recv.at[k, d - 1], lax.rem(me + 4 * d, n),
            )
            for d in range(1, peers)
        ]
        for k in range(2)
    ]
    for copy in v1:
        copy.start()
    density(far.at[Y], Y)
    for k, cs in enumerate(sides):
        v1[k].wait_recv()
        away = vacc[:, 1 - side, core, :, cs] + r1[:, 1 - side, :, cs]
        t2s[k] = away.reshape(peers * rows, nvir // 2).astype(t2s.dtype)
        v2[k].start()
    for k, cs in enumerate(sides):
        keep[k] = vacc[:, side, core, :, cs] + r1[:, side, :, cs]
    density(far.at[Z], Z)
    for k in range(2):
        v2[k].wait_recv()
        total = keep[k] + t2r[k].astype(jnp.float32).reshape(peers, rows, nvir // 2)
        keep[k] = total
        t3s[k] = total.astype(t3s.dtype)
        for copy in v3[k]:
            copy.start()
    density(far.at[S], S, last=True)
    for k, cs in enumerate(sides):
        result = keep[k, row]
        for d, copy in enumerate(v3[k]):
            copy.wait_recv()
            result = result + t3r[k, d].astype(jnp.float32)
        out_ref[:, cs] = result * (2.0 / (n * (2 * REACH + 1)))

    for copy in [e_mate, e_y, e_z, e_s, m_copy, *y_copy, *z_copy, *s_copy, *v1, *v2, *v3[0], *v3[1]]:
        copy.wait_send()


def per_device(n, three_index, occ_energy, vir_energy):
    count, nvir, naux = three_index.shape
    rows, peers = nvir // n, n // 4
    narrow = jnp.bfloat16 if rows % 16 == 0 else jnp.float32
    f32, bf16, dma = jnp.float32, jnp.bfloat16, pltpu.SemaphoreType.DMA
    pairs = 2 * REACH + 1
    vmem, hbm = pl.BlockSpec(memory_space=pltpu.VMEM), pl.BlockSpec(memory_space=pltpu.HBM)
    count_pieces = len(cuts(nvir))
    pieces = dma((count_pieces,))
    aux, vir = pl.pallas_call(
        functools.partial(kernel, n),
        out_shape=(jax.ShapeDtypeStruct((nvir, naux), bf16), jax.ShapeDtypeStruct((rows, nvir), f32)),
        in_specs=[hbm, pl.BlockSpec(memory_space=pltpu.SMEM), hbm],
        out_specs=(vmem, vmem),
        scratch_shapes=[
            pltpu.VMEM((nvir, naux), bf16),
            pltpu.VMEM((1, nvir), f32),
            pltpu.VMEM((nvir, naux), bf16),
            pltpu.VMEM((3, nvir, naux), bf16),
            pltpu.VMEM((pairs, 8, nvir), f32),
            pltpu.VMEM((nvir, nvir), f32),
            pltpu.VMEM((3, nvir, nvir), f32),
            pltpu.VMEM((3, nvir, nvir), bf16),
            pltpu.VMEM((3, nvir, nvir), bf16),
            pltpu.VMEM((nvir, naux), f32),
            pltpu.VMEM((peers, 2, 2, rows, nvir), f32),
            pltpu.VMEM((peers, 2, rows, nvir), f32),
            pltpu.VMEM((2, peers * rows, nvir // 2), bf16),
            pltpu.VMEM((2, peers * rows, nvir // 2), bf16),
            pltpu.VMEM((2, peers, rows, nvir // 2), f32),
            pltpu.VMEM((2, peers, rows, nvir // 2), narrow),
            pltpu.VMEM((2, peers - 1, rows, nvir // 2), narrow),
            dma((4,)), dma((4,)), dma, dma, pieces, pieces, pieces, pieces, pieces, pieces,
            dma((4,)), dma((4,)), dma((2, peers - 1)), dma((2, peers - 1)), dma((2,)),
        ],
        compiler_params=pltpu.CompilerParams(
            collective_id=0, has_side_effects=True, vmem_limit_bytes=62 * 2**20
        ),
        cost_estimate=pl.CostEstimate(
            flops=pairs * (4 * nvir * nvir * naux + 2 * nvir**3), bytes_accessed=4 * nvir * naux, transcendentals=0
        ),
    )(three_index.reshape(nvir, naux), occ_energy, vir_energy.reshape(1, nvir))
    return aux.reshape(three_index.shape), vir


def solution(mesh):
    placed = (P(("geom", "occ"), None, None), P(("geom", "occ")), P("geom"))
    return jax.shard_map(
        functools.partial(per_device, mesh.shape["occ"]),
        mesh=mesh,
        in_specs=placed,
        out_specs=(P(("geom", "occ"), None, None), P(("geom", "occ"), None)),
        check_vma=False,
    )
```
